32 devices in a mesh: row: 8 (over z, core), col: 4 (over y, x).
Axes of the slice: x: 2, y: 2, z: 4, core: 2. Of those that a mesh axis runs over, the one named last changes fastest.
Arguments:
- token_ids: int32 [16, 256], P('row'), may hold values from 0 to 16383
- passage_lengths: int32 [16], P('row'), may hold values from 64 to 256, as said below
- embedding: bfloat16 [16384, 4096], P(None, 'col'), may hold values from -8 to 8
- attn_gain: bfloat16 [4096], P('col'), may hold values from 0.25 to 1.75
- final_gain: bfloat16 [4096], P('col'), may hold values from 0.25 to 1.75
- query_weight: bfloat16 [4096, 4096], P('row', 'col'), may hold values from -0.5 to 0.5
- key_weight: bfloat16 [4096, 4096], P('row', 'col'), may hold values from -0.5 to 0.5
- value_weight: bfloat16 [4096, 4096], P('row', 'col'), may hold values from -0.09375 to 0.09375
- out_weight: bfloat16 [4096, 4096], P('row', 'col'), may hold values from -0.09375 to 0.09375
- crosskey_weight: bfloat16 [4096, 4096], P('row', 'col'), may hold values from -0.09375 to 0.09375
- crossvalue_weight: bfloat16 [4096, 4096], P('row', 'col'), may hold values from -0.09375 to 0.09375
Outputs:
- hidden_out: bfloat16 [4096, 4096], P('row', 'col')
- cross_keys: bfloat16 [4096, 16, 256], P('row', 'col')
- cross_values: bfloat16 [4096, 16, 256], P('row', 'col')
The draws below stay inside these ranges and needn't reach their ends.
Inputs may be any that keep to these rules, and one draw needn't show every extreme that they name: `passage_lengths`: some passage of every draw has all 256 slots valid.
All inputs are finite; a program needn't handle non-finite values.
Results may differ from the reference program's by a relative error of at most 0.0082.
Values may be sent and summed in bfloat16 or wider, within the bound.
A program may use at most 128 MiB of HBM per device.

```python
import math
import jax
import jax.numpy as jnp
import numpy as np
from jax import lax

D = 4096
HEADS = 16
HD = 256
VOCAB = 16384
PLEN = 256
PASSAGES = 16
TOKENS = 4096


def draw_passage_lengths(key, part):
    first_key = jax.random.fold_in(key, 11)
    second_key = jax.random.fold_in(key, 12)
    drawn = jax.random.randint(first_key, (PASSAGES,), PLEN // 4, PLEN + 1)
    chosen = jax.random.randint(second_key, (), 0, PASSAGES)
    return jnp.where(jnp.arange(PASSAGES) == chosen, PLEN, drawn).astype(jnp.int32)


def draw_embedding(key, part):
    base_key = jax.random.fold_in(key, 21)
    row_key = jax.random.fold_in(key, 22)
    col_key = jax.random.fold_in(key, 23)
    row_scale = jnp.exp(jax.random.uniform(row_key, (VOCAB, 1), jnp.float32, math.log(0.15), math.log(1.5)))
    rising = jnp.exp(math.log(3.0) * (jnp.arange(D, dtype=jnp.float32) / D - 0.5))
    col_scale = rising[None, :] * jnp.exp(jax.random.uniform(col_key, (1, D), jnp.float32, math.log(0.6), math.log(1.8)))
    values = jax.random.normal(base_key, (VOCAB, D), jnp.float32) * row_scale * col_scale
    return jnp.clip(values, -8.0, 8.0).astype(jnp.bfloat16)


def shared_projection(key, salt):
    own = jax.random.normal(jax.random.fold_in(key, salt), (D, D), jnp.float32) / math.sqrt(D)
    values = own
    return jnp.clip(values, -0.5, 0.5).astype(jnp.bfloat16)


def draw_query_weight(key, part):
    return shared_projection(key, 31)


def draw_key_weight(key, part):
    return shared_projection(key, 32)


def set_ends(entries, own_key, smallest, largest):
    longest = entries.shape.index(max(entries.shape))
    spots = []
    for shift in (0, 1):
        where = [jax.random.randint(jax.random.fold_in(own_key, axis), (), 0, length) for axis, length in enumerate(entries.shape)]
        where[longest] = (where[longest] + shift) % entries.shape[longest]
        spots.append(tuple(where))
    return entries.at[spots[0]].set(smallest).at[spots[1]].set(largest)


def shard_levels(stream_key, shape, shards, least, top_value):
    factor_of = 1.0
    for position, parts in shards:
        steps = jax.random.uniform(jax.random.fold_in(jax.random.fold_in(stream_key, 6), position), (parts,), jnp.float32, least / len(shards), top_value / len(shards))
        factor_of = factor_of * jnp.repeat(jnp.exp(steps), shape[position] // parts).reshape((-1,) + (1,) * (len(shape) - 1 - position))
    return factor_of


def cumulative_ranks(amount, slope):
    loads = [(1 << 20) // math.isqrt(standing ** slope) + 1 for standing in range(1, amount + 1)]
    scale = 1 + sum(loads) // (1 << 30)
    return np.cumsum(np.array([max(1, weight // scale) for weight in loads]))


def ranked(stream_key, dims, amount, lean):
    listing = cumulative_ranks(amount, lean)
    lot = jax.random.randint(jax.random.fold_in(stream_key, 1), dims, 0, int(listing[amount - 1]))
    grade = jnp.searchsorted(jnp.asarray(listing, jnp.int32), lot, side="right")
    return jax.random.permutation(jax.random.fold_in(stream_key, 2), amount)[grade].astype(jnp.int32)


def gaussian(key, shape, scale, bound, shards=(), kind=jnp.bfloat16):
    entries = scale * jax.random.normal(key, shape, jnp.float32)
    if shards:
        entries = entries * shard_levels(key, shape, shards, -0.22, 0.18)
    return jnp.clip(entries, -bound, bound).astype(kind)


def setup_inputs(seed: int = 0) -> dict:
    arg_keys = jax.random.split(jax.random.key(seed), 12)
    return {
        "token_ids": set_ends(ranked(arg_keys[0], (PASSAGES, PLEN), VOCAB, 2), jax.random.fold_in(arg_keys[0], 3), 0, VOCAB - 1).astype(jnp.int32),
        "passage_lengths": draw_passage_lengths(jax.random.fold_in(arg_keys[11], 71), 0),
        "embedding": draw_embedding(jax.random.fold_in(arg_keys[11], 71), 0),
        "attn_gain": jnp.clip(1.0 + 0.15 * jax.random.normal(arg_keys[3], (D,), jnp.float32), 0.25, 1.75).astype(jnp.bfloat16),
        "final_gain": jnp.clip(1.0 + 0.15 * jax.random.normal(arg_keys[4], (D,), jnp.float32), 0.25, 1.75).astype(jnp.bfloat16),
        "query_weight": draw_query_weight(jax.random.fold_in(arg_keys[11], 71), 0),
        "key_weight": draw_key_weight(jax.random.fold_in(arg_keys[11], 71), 0),
        "value_weight": gaussian(arg_keys[7], (D, D), D ** -0.5, 0.09375, ((0, 8), (1, 4))),
        "out_weight": gaussian(arg_keys[8], (D, D), D ** -0.5, 0.09375, ((0, 8), (1, 4))),
        "crosskey_weight": gaussian(arg_keys[9], (D, D), D ** -0.5, 0.09375, ((0, 8), (1, 4))),
        "crossvalue_weight": gaussian(arg_keys[10], (D, D), D ** -0.5, 0.09375, ((0, 8), (1, 4))),
    }


epsilon = 1e-06
masked_score = -1000000000.0

def rms_norm(row_block, gain_row):
    widened = row_block.astype(jnp.float32)
    mean_square = lax.optimization_barrier(jnp.mean(widened * widened, axis=1, keepdims=True))
    return (widened * lax.rsqrt(mean_square + epsilon) * gain_row.astype(jnp.float32)).astype(jnp.bfloat16)

def project(activ, weight):
    return jnp.dot(activ, weight, preferred_element_type=jnp.float32)

def reference(token_ids, passage_lengths, embedding, attn_gain, final_gain, query_weight, key_weight, value_weight, out_weight, crosskey_weight, crossvalue_weight):
    embedded = jnp.take(embedding, token_ids.reshape(-1), axis=0)
    normed = rms_norm(embedded, attn_gain)
    query_rows = project(normed, query_weight).astype(jnp.bfloat16)
    key_rows = project(normed, key_weight).astype(jnp.bfloat16)
    value_rows = project(normed, value_weight).astype(jnp.bfloat16)
    query_four = query_rows.astype(jnp.float32).reshape(PASSAGES, PLEN, HEADS, HD)
    key_four = key_rows.astype(jnp.float32).reshape(PASSAGES, PLEN, HEADS, HD)
    value_four = value_rows.astype(jnp.float32).reshape(PASSAGES, PLEN, HEADS, HD)
    scores = jnp.einsum('pihd,pjhd->phij', query_four, key_four) * HD ** (-0.5)
    valid = jnp.arange(PLEN, dtype=jnp.int32)[None, :] < passage_lengths[:, None]
    scores = jnp.where(valid[:, None, None, :], scores, masked_score)
    highest = lax.optimization_barrier(jnp.max(scores, axis=-1, keepdims=True))
    expon = jnp.exp(scores - highest)
    probs = (expon / lax.optimization_barrier(jnp.sum(expon, axis=-1, keepdims=True))).astype(jnp.bfloat16)
    attended = jnp.einsum('phij,pjhd->pihd', probs.astype(jnp.float32), value_four)
    attended = attended.astype(jnp.bfloat16).reshape(TOKENS, D)
    hidden_out = (embedded.astype(jnp.float32) + project(attended, out_weight)).astype(jnp.bfloat16)
    final_normed = rms_norm(hidden_out, final_gain)
    cross_keys = project(final_normed, crosskey_weight).astype(jnp.bfloat16).reshape(TOKENS, HEADS, HD)
    cross_values = project(final_normed, crossvalue_weight).astype(jnp.bfloat16).reshape(TOKENS, HEADS, HD)
    return (hidden_out, cross_keys, cross_values)
```

```python
import jax
import jax.numpy as jnp
import functools

from jax import lax
from jax.experimental import pallas as pl
from jax.experimental.pallas import tpu as pltpu
from jax.sharding import PartitionSpec as P

D = 4096
HD = 256
PLEN = 256


epsilon = 1e-06
masked_score = -1000000000.0


def scaled_rows(widened, summed, gain_row):
    inverse = lax.rsqrt(summed / D + epsilon)
    return (widened * inverse * gain_row.astype(jnp.float32)).astype(jnp.bfloat16)


def spread_norm(row_block, gain_row, which):
    if which == 0:
        gathered, gains = (
            lax.all_gather(row_block, "col", axis=1, tiled=True),
            lax.all_gather(gain_row.reshape(1, -1), "col", axis=1, tiled=True),
        )
    else:
        gathered, gains = (
            lax.all_gather(row_block, "col", axis=1, tiled=True),
            lax.all_gather(gain_row.reshape(1, -1), "col", axis=1, tiled=True),
        )
    widened = gathered.astype(jnp.float32)
    summed = jnp.sum(widened * widened, axis=1, keepdims=True)
    return scaled_rows(widened, summed, gains)


def add_terms(source, pieces):
    return tuple(
        (
            jnp.dot(source, weight_piece, preferred_element_type=jnp.float32)
            for weight_piece in pieces
        )
    )


def attend(query_rows, key_rows, value_rows, passage_lengths):
    tok_rows, local_width = query_rows.shape
    passages_here = tok_rows // PLEN
    heads_here = local_width // HD
    query_four = query_rows.reshape(passages_here, PLEN, heads_here, HD)
    key_four = key_rows.reshape(passages_here, PLEN, heads_here, HD)
    value_four = value_rows.reshape(passages_here, PLEN, heads_here, HD)
    scores = jnp.einsum(
        "pihd,pjhd->phij", query_four, key_four, preferred_element_type=jnp.float32
    ) * HD ** (-0.5)
    valid = jnp.arange(PLEN, dtype=jnp.int32)[None, :] < passage_lengths[:, None]
    scores = jnp.where(valid[:, None, None, :], scores, masked_score)
    highest = jnp.max(scores, axis=-1, keepdims=True)
    expon = jnp.exp(scores - highest)
    probs = (expon / jnp.sum(expon, axis=-1, keepdims=True)).astype(jnp.bfloat16)
    mixed = jnp.einsum("phij,pjhd->pihd", probs, value_four, preferred_element_type=jnp.float32)
    return mixed.astype(jnp.bfloat16).reshape(tok_rows, local_width)


def shards(
    token_ids,
    passage_lengths,
    embedding,
    attn_gain,
    final_gain,
    query_weight,
    key_weight,
    value_weight,
    out_weight,
    crosskey_weight,
    crossvalue_weight,
):
    embedded = jnp.take(embedding, token_ids.reshape(-1), axis=0)
    normed = spread_norm(embedded, attn_gain, 0)
    tok_rows = normed.shape[0]
    local_width = query_weight.shape[1]
    query_sum, key_sum, value_sum = add_terms(
        normed,
        (
            lax.all_gather(query_weight, "row", axis=0, tiled=True),
            lax.all_gather(key_weight, "row", axis=0, tiled=True),
            lax.all_gather(value_weight, "row", axis=0, tiled=True),
        ),
    )
    attended = attend(
        query_sum.astype(jnp.bfloat16),
        key_sum.astype(jnp.bfloat16),
        value_sum.astype(jnp.bfloat16),
        passage_lengths,
    )
    heads_full = lax.all_gather(attended, "col", axis=1, tiled=True)
    (projected,) = add_terms(heads_full, (lax.all_gather(out_weight, "row", axis=0, tiled=True),))
    hidden_out = (embedded.astype(jnp.float32) + projected).astype(jnp.bfloat16)
    final_normed = spread_norm(hidden_out, final_gain, 1)
    crosskey_sum, crossvalue_sum = add_terms(
        final_normed,
        (
            lax.all_gather(crosskey_weight, "row", axis=0, tiled=True),
            lax.all_gather(crossvalue_weight, "row", axis=0, tiled=True),
        ),
    )
    heads_here = local_width // HD
    cross_keys = crosskey_sum.astype(jnp.bfloat16).reshape(tok_rows, heads_here, HD)
    cross_values = crossvalue_sum.astype(jnp.bfloat16).reshape(tok_rows, heads_here, HD)
    return (hidden_out, cross_keys, cross_values)


def remote(source, target, send_sem, recv_sem, device):
    return pltpu.make_async_remote_copy(
        src_ref=source,
        dst_ref=target,
        send_sem=send_sem,
        recv_sem=recv_sem,
        device_id=device,
        device_id_type=pl.DeviceIdType.MESH,
    )


def place_here():
    row, col = lax.axis_index("row"), lax.axis_index("col")
    near = col + 1 - 2 * lax.rem(col, 2)
    far = lax.rem(col + 2, 4)
    return row, col, near, far


def greet(devices):
    barrier = pltpu.get_barrier_semaphore()
    for device in devices:
        pl.semaphore_signal(
            barrier, inc=1, device_id=device, device_id_type=pl.DeviceIdType.MESH
        )
    pl.semaphore_wait(barrier, len(devices))


def first_hop(item, block, place, sends, recvs):
    row, col, near, far = place_here()
    copies = [
        remote(block, place(col), sends.at[item, 0], recvs.at[item, 0], (row, near)),
        remote(block, place(col), sends.at[item, 1], recvs.at[item, 1], (row, far)),
    ]
    for copy in copies:
        copy.start()
    return copies


def second_hop(item, first, half, sends, recvs):
    row, col, near, far = place_here()
    first[0].wait_recv()
    upper = remote(
        half(near, 0), half(near, 0), sends.at[item, 2], recvs.at[item, 2], (row, far)
    )
    upper.start()
    first[1].wait_recv()
    lower = remote(
        half(far, 1), half(far, 1), sends.at[item, 3], recvs.at[item, 3], (row, near)
    )
    lower.start()
    return [upper, lower]


def settle(first, second):
    for copy in second:
        copy.wait()
    for copy in first:
        copy.wait_send()


def row_places(full_ref, start, rows, width):
    def place(col):
        return full_ref.at[pl.ds(start, rows), pl.ds(pl.multiple_of(col * width, width), width)]

    def half(col, which):
        return full_ref.at[
            pl.ds(start + which * (rows // 2), rows // 2),
            pl.ds(pl.multiple_of(col * width, width), width),
        ]

    return place, half


def spread_kernel(
    planes,
    parts,
    x_ref,
    q_ref,
    k_ref,
    v_ref,
    full_ref,
    weight_ref,
    local_sem,
    sends,
    recvs,
    plane_send,
    plane_recv,
    core_send,
    core_recv,
):
    row, col, near, far = place_here()
    plane, core = row // 2, lax.rem(row, 2)
    other = row + 1 - 2 * core
    others = [2 * lax.rem(plane + step, planes) + core for step in range(1, planes)]
    greet([(row, near), (row, far), (other, col)] + [(there, col) for there in others])

    rows, width = x_ref.shape
    depth = q_ref.shape[0]
    head_width = q_ref.shape[1] // planes
    chunk = rows // parts
    sources = (q_ref, k_ref, v_ref)

    def weight_rows(owner):
        return pl.ds(pl.multiple_of(owner * depth, depth), depth)

    def piece(which, target):
        return sources[which].at[
            :, pl.ds(pl.multiple_of(target * head_width, head_width), head_width)
        ]

    def slot(which, owner):
        return weight_ref.at[weight_rows(owner), pl.ds(which * head_width, head_width)]

    firsts, halves = [], []
    for part in range(parts):
        place, half = row_places(full_ref, part * chunk, chunk, width)
        firsts.append(
            first_hop(part, x_ref.at[pl.ds(part * chunk, chunk), :], place, sends, recvs)
        )
        halves.append(half)
    own = [
        pltpu.make_async_copy(piece(which, plane), slot(which, row), local_sem.at[which])
        for which in range(3)
    ]
    own.append(
        pltpu.make_async_copy(
            x_ref, full_ref.at[:, pl.ds(pl.multiple_of(col * width, width), width)], local_sem.at[3]
        )
    )
    for copy in own:
        copy.start()
    crossing = []
    for step in range(1, planes):
        target = lax.rem(plane + step, planes)
        crossing.append(
            [
                remote(
                    piece(which, target),
                    slot(which, row),
                    plane_send.at[step - 1, which],
                    plane_recv.at[step - 1, which],
                    (2 * target + core, col),
                )
                for which in range(3)
            ]
        )
        for copy in crossing[-1]:
            copy.start()
    seconds = []
    for part in range(parts):
        seconds.append(second_hop(part, firsts[part], halves[part], sends, recvs))
    shared = []
    for step in range(planes):
        if step == 0:
            for copy in own[:3]:
                copy.wait()
        else:
            for copy in crossing[step - 1]:
                copy.wait_recv()
        owner = 2 * lax.rem(plane + planes - step, planes) + core
        block = weight_ref.at[weight_rows(owner), :]
        shared.append(remote(block, block, core_send.at[step], core_recv.at[step], (other, col)))
        shared[-1].start()
    own[3].wait()
    for part in range(parts):
        settle(firsts[part], seconds[part])
    for group in crossing:
        for copy in group:
            copy.wait_send()
    for copy in shared:
        copy.wait()


def spread(x, weights, planes):
    rows, width = x.shape
    depth, columns = weights[0].shape
    parts = planes
    head_width = columns // planes
    return pl.pallas_call(
        functools.partial(spread_kernel, planes, parts),
        out_shape=(
            jax.ShapeDtypeStruct((rows, 4 * width), x.dtype),
            jax.ShapeDtypeStruct((2 * planes * depth, 3 * head_width), x.dtype),
        ),
        in_specs=[pl.BlockSpec(memory_space=pl.ANY)] * 4,
        out_specs=[pl.BlockSpec(memory_space=pl.ANY)] * 2,
        scratch_shapes=[
            pltpu.SemaphoreType.DMA((4,)),
            pltpu.SemaphoreType.DMA((parts, 4)),
            pltpu.SemaphoreType.DMA((parts, 4)),
            pltpu.SemaphoreType.DMA((planes - 1, 3)),
            pltpu.SemaphoreType.DMA((planes - 1, 3)),
            pltpu.SemaphoreType.DMA((planes,)),
            pltpu.SemaphoreType.DMA((planes,)),
        ],
        compiler_params=pltpu.CompilerParams(collective_id=0, has_side_effects=True),
        cost_estimate=pl.CostEstimate(
            flops=0, bytes_accessed=20 * rows * width * 2, transcendentals=0
        ),
    )(x, *weights)


def regroup_kernel(
    planes, att_ref, full_ref, local_sem, sends, recvs, plane_send, plane_recv
):
    row, col, near, far = place_here()
    plane, core = row // 2, lax.rem(row, 2)
    others = [2 * lax.rem(plane + step, planes) + core for step in range(1, planes)]
    greet([(row, near), (row, far)] + [(there, col) for there in others])

    rows, head_width = att_ref.shape
    rows = rows // planes
    width = head_width * planes

    def block(target):
        return att_ref.at[pl.ds(pl.multiple_of(target * rows, rows), rows), :]

    def places(source):
        def columns(where):
            return pl.ds(
                pl.multiple_of(where * width + source * head_width, head_width), head_width
            )

        def place(where):
            return full_ref.at[:, columns(where)]

        def half(where, which):
            return full_ref.at[pl.ds(which * (rows // 2), rows // 2), columns(where)]

        return place, half

    crossing = []
    for step in range(1, planes):
        target = lax.rem(plane + step, planes)
        crossing.append(
            remote(
                block(target),
                places(plane)[0](col),
                plane_send.at[step - 1],
                plane_recv.at[step - 1],
                (2 * target + core, col),
            )
        )
        crossing[-1].start()
    own = pltpu.make_async_copy(block(plane), places(plane)[0](col), local_sem.at[0])
    own.start()
    firsts, halves = [], []
    for step in range(planes):
        place, half = places(lax.rem(plane + planes - step, planes))
        if step > 0:
            crossing[step - 1].wait_recv()
            start = place(col)
        else:
            start = block(plane)
        firsts.append(first_hop(step, start, place, sends, recvs))
        halves.append(half)
    seconds = []
    for step in range(planes):
        seconds.append(second_hop(step, firsts[step], halves[step], sends, recvs))
    own.wait()
    for step in range(planes):
        settle(firsts[step], seconds[step])
    for copy in crossing:
        copy.wait_send()


def regroup(attended, planes):
    rows, head_width = attended.shape
    return pl.pallas_call(
        functools.partial(regroup_kernel, planes),
        out_shape=jax.ShapeDtypeStruct(
            (rows // planes, 4 * planes * head_width), attended.dtype
        ),
        in_specs=[pl.BlockSpec(memory_space=pl.ANY)],
        out_specs=pl.BlockSpec(memory_space=pl.ANY),
        scratch_shapes=[
            pltpu.SemaphoreType.DMA((1,)),
            pltpu.SemaphoreType.DMA((planes, 4)),
            pltpu.SemaphoreType.DMA((planes, 4)),
            pltpu.SemaphoreType.DMA((planes - 1,)),
            pltpu.SemaphoreType.DMA((planes - 1,)),
        ],
        compiler_params=pltpu.CompilerParams(collective_id=1, has_side_effects=True),
        cost_estimate=pl.CostEstimate(
            flops=0, bytes_accessed=40 * rows * head_width * 2, transcendentals=0
        ),
    )(attended)


def widen_kernel(parts, x_ref, full_ref, local_sem, sends, recvs):
    row, col, near, far = place_here()
    greet([(row, near), (row, far)])
    rows, width = x_ref.shape
    chunk = rows // parts
    firsts, halves = [], []
    for part in range(parts):
        place, half = row_places(full_ref, part * chunk, chunk, width)
        firsts.append(
            first_hop(part, x_ref.at[pl.ds(part * chunk, chunk), :], place, sends, recvs)
        )
        halves.append(half)
    own = pltpu.make_async_copy(
        x_ref, full_ref.at[:, pl.ds(pl.multiple_of(col * width, width), width)], local_sem.at[0]
    )
    own.start()
    seconds = []
    for part in range(parts):
        seconds.append(second_hop(part, firsts[part], halves[part], sends, recvs))
    own.wait()
    for part in range(parts):
        settle(firsts[part], seconds[part])


def widen(x, parts=4):
    rows, width = x.shape
    return pl.pallas_call(
        functools.partial(widen_kernel, parts),
        out_shape=jax.ShapeDtypeStruct((rows, 4 * width), x.dtype),
        in_specs=[pl.BlockSpec(memory_space=pl.ANY)],
        out_specs=pl.BlockSpec(memory_space=pl.ANY),
        scratch_shapes=[
            pltpu.SemaphoreType.DMA((1,)),
            pltpu.SemaphoreType.DMA((parts, 4)),
            pltpu.SemaphoreType.DMA((parts, 4)),
        ],
        compiler_params=pltpu.CompilerParams(collective_id=2, has_side_effects=True),
        cost_estimate=pl.CostEstimate(
            flops=0, bytes_accessed=20 * rows * width * 2, transcendentals=0
        ),
    )(x)


def norm_rows(gathered, gains):
    widened = gathered.astype(jnp.float32)
    summed = jnp.sum(widened * widened, axis=1, keepdims=True)
    return scaled_rows(widened, summed, gains)


def plane_shards(
    planes,
    token_ids,
    passage_lengths,
    embedding,
    attn_gain,
    final_gain,
    query_weight,
    key_weight,
    value_weight,
    out_weight,
    crosskey_weight,
    crossvalue_weight,
):
    row = lax.axis_index("row")
    plane, core = row // 2, row % 2
    tok_rows = token_ids.size
    local_width = query_weight.shape[1]
    facts = jnp.concatenate([token_ids.reshape(-1), passage_lengths])
    facts = lax.all_gather(facts, "row", axis=0).reshape(planes, 2, -1)
    facts = lax.dynamic_index_in_dim(facts, core, axis=1, keepdims=False)
    ids, lengths = facts[:, :tok_rows].reshape(-1), facts[:, tok_rows:].reshape(-1)
    gains = lax.all_gather(jnp.concatenate([attn_gain, final_gain]), "col", axis=0)
    gains = gains.reshape(4, 2, -1).transpose(1, 0, 2).reshape(2, 1, -1)

    embedded_all = jnp.take(embedding, ids, axis=0)
    embedded = lax.dynamic_slice_in_dim(embedded_all, plane * tok_rows, tok_rows, axis=0)
    gathered, weight = spread(embedded_all, (query_weight, key_weight, value_weight), planes)
    normed = norm_rows(gathered, gains[0])
    (sums,) = add_terms(normed, (weight,))
    sums = sums.astype(jnp.bfloat16)
    part = local_width // planes
    attended = attend(sums[:, :part], sums[:, part : 2 * part], sums[:, 2 * part :], lengths)
    heads_full = regroup(attended, planes)
    (projected,) = add_terms(heads_full, (lax.all_gather(out_weight, "row", axis=0, tiled=True),))
    hidden_out = (embedded.astype(jnp.float32) + projected).astype(jnp.bfloat16)
    final_normed = norm_rows(widen(hidden_out), gains[1])
    crosskey_sum, crossvalue_sum = add_terms(
        final_normed,
        (
            lax.all_gather(crosskey_weight, "row", axis=0, tiled=True),
            lax.all_gather(crossvalue_weight, "row", axis=0, tiled=True),
        ),
    )
    heads_here = local_width // HD
    cross_keys = crosskey_sum.astype(jnp.bfloat16).reshape(tok_rows, heads_here, HD)
    cross_values = crossvalue_sum.astype(jnp.bfloat16).reshape(tok_rows, heads_here, HD)
    return (hidden_out, cross_keys, cross_values)


def any_shards(mesh):
    rows, cols = mesh.shape["row"], mesh.shape["col"]
    planes = rows // 2
    heads_here = D // HD // cols
    if cols == 4 and rows % 2 == 0 and planes > 1 and heads_here % planes == 0:
        return functools.partial(plane_shards, planes)
    return shards


def solution(mesh):
    return jax.shard_map(
        any_shards(mesh),
        mesh=mesh,
        in_specs=(
            P("row", None),
            P("row"),
            P(None, "col"),
            P("col"),
            P("col"),
            P("row", "col"),
            P("row", "col"),
            P("row", "col"),
            P("row", "col"),
            P("row", "col"),
            P("row", "col"),
        ),
        out_specs=(P("row", "col"), P("row", "col", None), P("row", "col", None)),
        check_vma=False,
    )
```

```python
import jax
import jax.numpy as jnp
import functools

from jax import lax
from jax.experimental import pallas as pl
from jax.experimental.pallas import tpu as pltpu
from jax.sharding import PartitionSpec as P

D = 4096
HD = 256
PLEN = 256


epsilon = 1e-06
masked_score = -1000000000.0


def scaled_rows(widened, summed, gain_row):
    inverse = lax.rsqrt(summed / D + epsilon)
    return (widened * inverse * gain_row.astype(jnp.float32)).astype(jnp.bfloat16)


def spread_norm(row_block, gain_row, which):
    if which == 0:
        gathered, gains = (
            lax.all_gather(row_block, "col", axis=1, tiled=True),
            lax.all_gather(gain_row.reshape(1, -1), "col", axis=1, tiled=True),
        )
    else:
        gathered, gains = (
            lax.all_gather(row_block, "col", axis=1, tiled=True),
            lax.all_gather(gain_row.reshape(1, -1), "col", axis=1, tiled=True),
        )
    widened = gathered.astype(jnp.float32)
    summed = jnp.sum(widened * widened, axis=1, keepdims=True)
    return scaled_rows(widened, summed, gains)


def add_terms(source, pieces):
    return tuple(
        (
            jnp.dot(source, weight_piece, preferred_element_type=jnp.float32)
            for weight_piece in pieces
        )
    )


def attend(query_rows, key_rows, value_rows, passage_lengths):
    tok_rows, local_width = query_rows.shape
    passages_here = tok_rows // PLEN
    heads_here = local_width // HD
    query_four = query_rows.reshape(passages_here, PLEN, heads_here, HD)
    key_four = key_rows.reshape(passages_here, PLEN, heads_here, HD)
    value_four = value_rows.reshape(passages_here, PLEN, heads_here, HD)
    scores = jnp.einsum(
        "pihd,pjhd->phij", query_four, key_four, preferred_element_type=jnp.float32
    ) * HD ** (-0.5)
    valid = jnp.arange(PLEN, dtype=jnp.int32)[None, :] < passage_lengths[:, None]
    scores = jnp.where(valid[:, None, None, :], scores, masked_score)
    highest = jnp.max(scores, axis=-1, keepdims=True)
    expon = jnp.exp(scores - highest)
    probs = (expon / jnp.sum(expon, axis=-1, keepdims=True)).astype(jnp.bfloat16)
    mixed = jnp.einsum("phij,pjhd->pihd", probs, value_four, preferred_element_type=jnp.float32)
    return mixed.astype(jnp.bfloat16).reshape(tok_rows, local_width)


def shards(
    token_ids,
    passage_lengths,
    embedding,
    attn_gain,
    final_gain,
    query_weight,
    key_weight,
    value_weight,
    out_weight,
    crosskey_weight,
    crossvalue_weight,
):
    embedded = jnp.take(embedding, token_ids.reshape(-1), axis=0)
    normed = spread_norm(embedded, attn_gain, 0)
    tok_rows = normed.shape[0]
    local_width = query_weight.shape[1]
    query_sum, key_sum, value_sum = add_terms(
        normed,
        (
            lax.all_gather(query_weight, "row", axis=0, tiled=True),
            lax.all_gather(key_weight, "row", axis=0, tiled=True),
            lax.all_gather(value_weight, "row", axis=0, tiled=True),
        ),
    )
    attended = attend(
        query_sum.astype(jnp.bfloat16),
        key_sum.astype(jnp.bfloat16),
        value_sum.astype(jnp.bfloat16),
        passage_lengths,
    )
    heads_full = lax.all_gather(attended, "col", axis=1, tiled=True)
    (projected,) = add_terms(heads_full, (lax.all_gather(out_weight, "row", axis=0, tiled=True),))
    hidden_out = (embedded.astype(jnp.float32) + projected).astype(jnp.bfloat16)
    final_normed = spread_norm(hidden_out, final_gain, 1)
    crosskey_sum, crossvalue_sum = add_terms(
        final_normed,
        (
            lax.all_gather(crosskey_weight, "row", axis=0, tiled=True),
            lax.all_gather(crossvalue_weight, "row", axis=0, tiled=True),
        ),
    )
    heads_here = local_width // HD
    cross_keys = crosskey_sum.astype(jnp.bfloat16).reshape(tok_rows, heads_here, HD)
    cross_values = crossvalue_sum.astype(jnp.bfloat16).reshape(tok_rows, heads_here, HD)
    return (hidden_out, cross_keys, cross_values)


def remote(source, target, send_sem, recv_sem, device):
    return pltpu.make_async_remote_copy(
        src_ref=source,
        dst_ref=target,
        send_sem=send_sem,
        recv_sem=recv_sem,
        device_id=device,
        device_id_type=pl.DeviceIdType.MESH,
    )


def place_here():
    row, col = lax.axis_index("row"), lax.axis_index("col")
    near = col + 1 - 2 * lax.rem(col, 2)
    far = lax.rem(col + 2, 4)
    return row, col, near, far


def greet(devices):
    barrier = pltpu.get_barrier_semaphore()
    for device in devices:
        pl.semaphore_signal(
            barrier, inc=1, device_id=device, device_id_type=pl.DeviceIdType.MESH
        )
    pl.semaphore_wait(barrier, len(devices))


def first_hop(item, block, place, sends, recvs):
    row, col, near, far = place_here()
    copies = [
        remote(block, place(col), sends.at[item, 0], recvs.at[item, 0], (row, near)),
        remote(block, place(col), sends.at[item, 1], recvs.at[item, 1], (row, far)),
    ]
    for copy in copies:
        copy.start()
    return copies


def second_hop(item, first, half, sends, recvs):
    row, col, near, far = place_here()
    first[0].wait_recv()
    upper = remote(
        half(near, 0), half(near, 0), sends.at[item, 2], recvs.at[item, 2], (row, far)
    )
    upper.start()
    first[1].wait_recv()
    lower = remote(
        half(far, 1), half(far, 1), sends.at[item, 3], recvs.at[item, 3], (row, near)
    )
    lower.start()
    return [upper, lower]


def settle(first, second):
    for copy in second:
        copy.wait()
    for copy in first:
        copy.wait_send()


def row_places(full_ref, start, rows, width):
    def place(col):
        return full_ref.at[pl.ds(start, rows), pl.ds(pl.multiple_of(col * width, width), width)]

    def half(col, which):
        return full_ref.at[
            pl.ds(start + which * (rows // 2), rows // 2),
            pl.ds(pl.multiple_of(col * width, width), width),
        ]

    return place, half


def spread_kernel(
    planes,
    parts,
    x_ref,
    q_ref,
    k_ref,
    v_ref,
    full_ref,
    weight_ref,
    local_sem,
    sends,
    recvs,
    plane_send,
    plane_recv,
    core_send,
    core_recv,
):
    row, col, near, far = place_here()
    plane, core = row // 2, lax.rem(row, 2)
    other = row + 1 - 2 * core
    others = [2 * lax.rem(plane + step, planes) + core for step in range(1, planes)]
    greet([(row, near), (row, far), (other, col)] + [(there, col) for there in others])

    rows, width = x_ref.shape
    depth = q_ref.shape[0]
    head_width = q_ref.shape[1] // planes
    chunk = rows // parts
    sources = (q_ref, k_ref, v_ref)

    def weight_rows(owner):
        return pl.ds(pl.multiple_of(owner * depth, depth), depth)

    def piece(which, target):
        return sources[which].at[
            :, pl.ds(pl.multiple_of(target * head_width, head_width), head_width)
        ]

    def slot(which, owner):
        return weight_ref.at[weight_rows(owner), pl.ds(which * head_width, head_width)]

    firsts, halves = [], []
    for part in range(parts):
        place, half = row_places(full_ref, part * chunk, chunk, width)
        firsts.append(
            first_hop(part, x_ref.at[pl.ds(part * chunk, chunk), :], place, sends, recvs)
        )
        halves.append(half)
    own = [
        pltpu.make_async_copy(piece(which, plane), slot(which, row), local_sem.at[which])
        for which in range(3)
    ]
    own.append(
        pltpu.make_async_copy(
            x_ref, full_ref.at[:, pl.ds(pl.multiple_of(col * width, width), width)], local_sem.at[3]
        )
    )
    for copy in own:
        copy.start()
    crossing = []
    for step in range(1, planes):
        target = lax.rem(plane + step, planes)
        crossing.append(
            [
                remote(
                    piece(which, target),
                    slot(which, row),
                    plane_send.at[step - 1, which],
                    plane_recv.at[step - 1, which],
                    (2 * target + core, col),
                )
                for which in range(3)
            ]
        )
        for copy in crossing[-1]:
            copy.start()
    seconds = []
    for part in range(parts):
        seconds.append(second_hop(part, firsts[part], halves[part], sends, recvs))
    shared = []
    for step in range(planes):
        if step == 0:
            for copy in own[:3]:
                copy.wait()
        else:
            for copy in crossing[step - 1]:
                copy.wait_recv()
        owner = 2 * lax.rem(plane + planes - step, planes) + core
        block = weight_ref.at[weight_rows(owner), :]
        shared.append(remote(block, block, core_send.at[step], core_recv.at[step], (other, col)))
        shared[-1].start()
    own[3].wait()
    for part in range(parts):
        settle(firsts[part], seconds[part])
    for group in crossing:
        for copy in group:
            copy.wait_send()
    for copy in shared:
        copy.wait()


def spread(x, weights, planes):
    rows, width = x.shape
    depth, columns = weights[0].shape
    parts = planes
    head_width = columns // planes
    return pl.pallas_call(
        functools.partial(spread_kernel, planes, parts),
        out_shape=(
            jax.ShapeDtypeStruct((rows, 4 * width), x.dtype),
            jax.ShapeDtypeStruct((2 * planes * depth, 3 * head_width), x.dtype),
        ),
        in_specs=[pl.BlockSpec(memory_space=pl.ANY)] * 4,
        out_specs=[pl.BlockSpec(memory_space=pl.ANY)] * 2,
        scratch_shapes=[
            pltpu.SemaphoreType.DMA((4,)),
            pltpu.SemaphoreType.DMA((parts, 4)),
            pltpu.SemaphoreType.DMA((parts, 4)),
            pltpu.SemaphoreType.DMA((planes - 1, 3)),
            pltpu.SemaphoreType.DMA((planes - 1, 3)),
            pltpu.SemaphoreType.DMA((planes,)),
            pltpu.SemaphoreType.DMA((planes,)),
        ],
        compiler_params=pltpu.CompilerParams(collective_id=0, has_side_effects=True),
        cost_estimate=pl.CostEstimate(
            flops=0, bytes_accessed=20 * rows * width * 2, transcendentals=0
        ),
    )(x, *weights)


def regroup_kernel(
    planes, att_ref, full_ref, local_sem, sends, recvs, plane_send, plane_recv
):
    row, col, near, far = place_here()
    plane, core = row // 2, lax.rem(row, 2)
    others = [2 * lax.rem(plane + step, planes) + core for step in range(1, planes)]
    greet([(row, near), (row, far)] + [(there, col) for there in others])

    rows, head_width = att_ref.shape
    rows = rows // planes
    width = head_width * planes

    def block(target):
        return att_ref.at[pl.ds(pl.multiple_of(target * rows, rows), rows), :]

    def places(source):
        def columns(where):
            return pl.ds(
                pl.multiple_of(where * width + source * head_width, head_width), head_width
            )

        def place(where):
            return full_ref.at[:, columns(where)]

        def half(where, which):
            return full_ref.at[pl.ds(which * (rows // 2), rows // 2), columns(where)]

        return place, half

    crossing = []
    for step in range(1, planes):
        target = lax.rem(plane + step, planes)
        crossing.append(
            remote(
                block(target),
                places(plane)[0](col),
                plane_send.at[step - 1],
                plane_recv.at[step - 1],
                (2 * target + core, col),
            )
        )
        crossing[-1].start()
    own = pltpu.make_async_copy(block(plane), places(plane)[0](col), local_sem.at[0])
    own.start()
    firsts, halves = [], []
    for step in range(planes):
        place, half = places(lax.rem(plane + planes - step, planes))
        if step > 0:
            crossing[step - 1].wait_recv()
            start = place(col)
        else:
            start = block(plane)
        firsts.append(first_hop(step, start, place, sends, recvs))
        halves.append(half)
    seconds = []
    for step in range(planes):
        seconds.append(second_hop(step, firsts[step], halves[step], sends, recvs))
    own.wait()
    for step in range(planes):
        settle(firsts[step], seconds[step])
    for copy in crossing:
        copy.wait_send()


def regroup(attended, planes):
    rows, head_width = attended.shape
    return pl.pallas_call(
        functools.partial(regroup_kernel, planes),
        out_shape=jax.ShapeDtypeStruct(
            (rows // planes, 4 * planes * head_width), attended.dtype
        ),
        in_specs=[pl.BlockSpec(memory_space=pl.ANY)],
        out_specs=pl.BlockSpec(memory_space=pl.ANY),
        scratch_shapes=[
            pltpu.SemaphoreType.DMA((1,)),
            pltpu.SemaphoreType.DMA((planes, 4)),
            pltpu.SemaphoreType.DMA((planes, 4)),
            pltpu.SemaphoreType.DMA((planes - 1,)),
            pltpu.SemaphoreType.DMA((planes - 1,)),
        ],
        compiler_params=pltpu.CompilerParams(collective_id=1, has_side_effects=True),
        cost_estimate=pl.CostEstimate(
            flops=0, bytes_accessed=40 * rows * head_width * 2, transcendentals=0
        ),
    )(attended)


def widen_kernel(parts, x_ref, full_ref, local_sem, sends, recvs):
    row, col, near, far = place_here()
    greet([(row, near), (row, far)])
    rows, width = x_ref.shape
    chunk = rows // parts
    firsts, halves = [], []
    for part in range(parts):
        place, half = row_places(full_ref, part * chunk, chunk, width)
        firsts.append(
            first_hop(part, x_ref.at[pl.ds(part * chunk, chunk), :], place, sends, recvs)
        )
        halves.append(half)
    own = pltpu.make_async_copy(
        x_ref, full_ref.at[:, pl.ds(pl.multiple_of(col * width, width), width)], local_sem.at[0]
    )
    own.start()
    seconds = []
    for part in range(parts):
        seconds.append(second_hop(part, firsts[part], halves[part], sends, recvs))
    own.wait()
    for part in range(parts):
        settle(firsts[part], seconds[part])


def widen(x, parts=4):
    rows, width = x.shape
    return pl.pallas_call(
        functools.partial(widen_kernel, parts),
        out_shape=jax.ShapeDtypeStruct((rows, 4 * width), x.dtype),
        in_specs=[pl.BlockSpec(memory_space=pl.ANY)],
        out_specs=pl.BlockSpec(memory_space=pl.ANY),
        scratch_shapes=[
            pltpu.SemaphoreType.DMA((1,)),
            pltpu.SemaphoreType.DMA((parts, 4)),
            pltpu.SemaphoreType.DMA((parts, 4)),
        ],
        compiler_params=pltpu.CompilerParams(collective_id=2, has_side_effects=True),
        cost_estimate=pl.CostEstimate(
            flops=0, bytes_accessed=20 * rows * width * 2, transcendentals=0
        ),
    )(x)


def announce_kernel(
    planes, fact_ref, gain_ref, facts_ref, gains_ref, local_sem, sends, recvs, gain_send, gain_recv
):
    row, col, near, far = place_here()
    plane, core = row // 2, lax.rem(row, 2)
    rows = [(2 * lax.rem(plane + step, planes) + core, col) for step in range(1, planes)]
    cols = [(row, near), (row, far), (row, 3 - col)]
    greet(rows + cols)
    tall, deep = fact_ref.shape[0], gain_ref.shape[0]
    fact_slot = facts_ref.at[pl.ds(pl.multiple_of(plane * tall, tall), tall), :]
    gain_slot = gains_ref.at[pl.ds(pl.multiple_of(col * deep, deep), deep), :]
    copies = [
        remote(fact_ref, fact_slot, sends.at[item], recvs.at[item], device)
        for item, device in enumerate(rows)
    ]
    copies += [
        remote(gain_ref, gain_slot, gain_send.at[item], gain_recv.at[item], device)
        for item, device in enumerate(cols)
    ]
    copies += [
        pltpu.make_async_copy(fact_ref, fact_slot, local_sem.at[0]),
        pltpu.make_async_copy(gain_ref, gain_slot, local_sem.at[1]),
    ]
    for copy in copies:
        copy.start()
    for copy in copies:
        copy.wait()


def announce(token_ids, passage_lengths, attn_gain, final_gain, planes):
    facts = jnp.concatenate([token_ids.reshape(-1), passage_lengths])
    used = facts.shape[0]
    facts = jnp.pad(facts, (0, -used % 1024)).reshape(-1, 128)
    gains = jnp.concatenate([attn_gain, final_gain])
    width = gains.shape[0]
    gains = jnp.pad(gains, (0, -width % 2048)).reshape(-1, 128)
    facts, gains = pl.pallas_call(
        functools.partial(announce_kernel, planes),
        out_shape=(
            jax.ShapeDtypeStruct((planes * facts.shape[0], 128), facts.dtype),
            jax.ShapeDtypeStruct((4 * gains.shape[0], 128), gains.dtype),
        ),
        in_specs=[pl.BlockSpec(memory_space=pl.ANY)] * 2,
        out_specs=[pl.BlockSpec(memory_space=pl.ANY)] * 2,
        scratch_shapes=[
            pltpu.SemaphoreType.DMA((2,)),
            pltpu.SemaphoreType.DMA((planes - 1,)),
            pltpu.SemaphoreType.DMA((planes - 1,)),
            pltpu.SemaphoreType.DMA((3,)),
            pltpu.SemaphoreType.DMA((3,)),
        ],
        compiler_params=pltpu.CompilerParams(collective_id=3, has_side_effects=True),
    )(facts, gains)
    facts = facts.reshape(planes, -1)
    gains = gains.reshape(4, -1)[:, :width].reshape(4, 2, -1)
    return (
        facts[:, : token_ids.size].reshape(-1),
        facts[:, token_ids.size : used].reshape(-1),
        gains.transpose(1, 0, 2).reshape(2, 1, -1),
    )


def norm_rows(gathered, gains):
    widened = gathered.astype(jnp.float32)
    summed = jnp.sum(widened * widened, axis=1, keepdims=True)
    return scaled_rows(widened, summed, gains)


def plane_shards(
    planes,
    token_ids,
    passage_lengths,
    embedding,
    attn_gain,
    final_gain,
    query_weight,
    key_weight,
    value_weight,
    out_weight,
    crosskey_weight,
    crossvalue_weight,
):
    row = lax.axis_index("row")
    plane = row // 2
    tok_rows = token_ids.size
    local_width = query_weight.shape[1]
    ids, lengths, gains = announce(token_ids, passage_lengths, attn_gain, final_gain, planes)
    embedded_all = jnp.take(embedding, ids, axis=0, mode="clip")
    embedded = lax.dynamic_slice_in_dim(embedded_all, plane * tok_rows, tok_rows, axis=0)
    gathered, weight = spread(embedded_all, (query_weight, key_weight, value_weight), planes)
    normed = norm_rows(gathered, gains[0])
    (sums,) = add_terms(normed, (weight,))
    sums = sums.astype(jnp.bfloat16)
    part = local_width // planes
    attended = attend(sums[:, :part], sums[:, part : 2 * part], sums[:, 2 * part :], lengths)
    heads_full = regroup(attended, planes)
    (projected,) = add_terms(heads_full, (lax.all_gather(out_weight, "row", axis=0, tiled=True),))
    hidden_out = (embedded.astype(jnp.float32) + projected).astype(jnp.bfloat16)
    final_normed = norm_rows(widen(hidden_out), gains[1])
    crosskey_sum, crossvalue_sum = add_terms(
        final_normed,
        (
            lax.all_gather(crosskey_weight, "row", axis=0, tiled=True),
            lax.all_gather(crossvalue_weight, "row", axis=0, tiled=True),
        ),
    )
    heads_here = local_width // HD
    cross_keys = crosskey_sum.astype(jnp.bfloat16).reshape(tok_rows, heads_here, HD)
    cross_values = crossvalue_sum.astype(jnp.bfloat16).reshape(tok_rows, heads_here, HD)
    return (hidden_out, cross_keys, cross_values)


def any_shards(mesh):
    rows, cols = mesh.shape["row"], mesh.shape["col"]
    planes = rows // 2
    heads_here = D // HD // cols
    if cols == 4 and rows % 2 == 0 and planes > 1 and heads_here % planes == 0:
        return functools.partial(plane_shards, planes)
    return shards


def solution(mesh):
    return jax.shard_map(
        any_shards(mesh),
        mesh=mesh,
        in_specs=(
            P("row", None),
            P("row"),
            P(None, "col"),
            P("col"),
            P("col"),
            P("row", "col"),
            P("row", "col"),
            P("row", "col"),
            P("row", "col"),
            P("row", "col"),
            P("row", "col"),
        ),
        out_specs=(P("row", "col"), P("row", "col", None), P("row", "col", None)),
        check_vma=False,
    )
```
